512 devices in a mesh: learn: 16 (over z), tp: 8 (over y_hi, x), rep: 4 (over y_lo, core).
Axes of the slice: x: 4, y: 4 (y_hi: 2, y_lo: 2; y = y_hi * 2 + y_lo), z: 16, core: 2. Of those that a mesh axis runs over, the one named last changes fastest.
Arguments:
- master: float32 [8192, 2048], P(('learn', 'rep'), 'tp'), may hold values from -0.0625 to 0.0625
- moment_one: float32 [8192, 2048], P(('learn', 'rep'), 'tp'), may hold values from -3 to 3
- moment_two: float32 [8192, 2048], P(('learn', 'rep'), 'tp'), may hold values from 0.25 to 4
- gradient: bfloat16 [8192, 2048], P(('learn', 'rep'), 'tp'), may hold values from -6 to 6
- hidden: bfloat16 [128, 4, 8192], P(('learn', 'rep'), None, 'tp'), may hold values from -12 to 12
- queries: bfloat16 [128, 4, 8192], P(('learn', 'rep'), None, 'tp'), may hold values from -135 to 135
- cache_keys: bfloat16 [128, 2048, 1024], P(('learn', 'rep'), None, 'tp'), may hold values from -4.5 to 4.5
- cache_values: bfloat16 [128, 2048, 1024], P(('learn', 'rep'), None, 'tp'), may hold values from -6 to 6
- lengths: int32 [128], P(('learn', 'rep')), may hold values from 512 to 2048
Outputs:
- new_master: float32 [8192, 2048], P(('learn', 'rep'), 'tp')
- new_moment_one: float32 [8192, 2048], P(('learn', 'rep'), 'tp')
- new_moment_two: float32 [8192, 2048], P(('learn', 'rep'), 'tp')
- fresh_kv: bfloat16 [128, 4, 2048], P(('learn', 'rep'), None, 'tp')
- attended: bfloat16 [128, 4, 8192], P(('learn', 'rep'), None, 'tp')
The draws below stay inside these ranges and needn't reach their ends.
All inputs are finite; a program needn't handle non-finite values.
Results may differ from the reference program's by a relative error of at most 0.014.
Values may be sent and summed in bfloat16 or wider, within the bound.
No kernel may reach another device: no remote copies, remote signals or barrier semaphores. Data moves between devices by JAX's collectives and lax.ppermute only.
A program may use at most 64 MiB of HBM per device.

```python
import math
import jax
import jax.numpy as jnp
from jax import lax

D = 8192
H = 64
KVH = 8
HD = 128
STEPS = 4
CTX = 2048
BATCH = 128


def shared_keys(key):
    normal_keys = jnp.clip(jax.random.normal(key, (BATCH, CTX, KVH * HD), jnp.float32), -4.5, 4.5)
    return normal_keys


def draw_cache_keys(key, part):
    normal_keys = shared_keys(key)
    return normal_keys.astype(jnp.bfloat16)


def draw_queries(key, part):
    key = jax.random.fold_in(key, 2)
    query_values = jnp.clip(jax.random.normal(key, (BATCH, STEPS, H * HD), jnp.float32), -4.5, 4.5)
    return query_values.astype(jnp.bfloat16)


def draw_lengths(key, part):
    key = jax.random.fold_in(key, 3)
    filled = jax.random.randint(key, (BATCH,), CTX // 4, CTX + 1, jnp.int32)
    filled = filled.at[0].set(CTX)
    filled = filled.at[1].set(CTX // 4)
    return filled


def steps_of(key, extent, pieces, low, high):
    loudness, own = 1.0, jax.random.fold_in(key, 6)
    for position, parts in pieces:
        steps = jnp.exp(jax.random.uniform(jax.random.fold_in(own, position), (parts,), jnp.float32, low / len(pieces), high / len(pieces)))
        loudness = loudness * jnp.repeat(steps, extent[position] // parts).reshape([-1 if axis == position else 1 for axis in range(len(extent))])
    return loudness


def bell_draw(key, extent, scale, reach, cuts=(), dtype=jnp.bfloat16):
    gain = steps_of(key, extent, cuts, -0.22, 0.18) if cuts else 1.0
    values = jax.random.normal(key, extent, jnp.float32) * scale * gain
    return jnp.minimum(jnp.maximum(values, -reach), reach).astype(dtype)


def setup_inputs(seed: int = 0) -> dict:
    key_of = jax.random.split(jax.random.key(seed), 10)
    master = bell_draw(key_of[0], (D, 2 * KVH * HD), D ** -0.5, 0.0625, ((0, 64), (1, 8)), jnp.float32)
    moment_one = bell_draw(key_of[1], (D, 2 * KVH * HD), 0.5, 3.0, ((0, 64), (1, 8)), jnp.float32)
    moment_two = jnp.clip(jnp.exp(math.log(4.0) - 2.7725887 * jax.random.uniform(key_of[2], (D, 2 * KVH * HD), jnp.float32) ** steps_of(key_of[2], (D, 2 * KVH * HD), ((0, 64), (1, 8)), -0.2, 0.2)), 0.25, 4.0)
    gradient = bell_draw(key_of[3], (D, 2 * KVH * HD), 1.0, 6.0, ((0, 64), (1, 8)))
    hidden = bell_draw(key_of[4], (BATCH, STEPS, D), 3.0, 12.0, ((0, 64), (2, 8)))
    queries = draw_queries(jax.random.fold_in(key_of[9], 71), 0)
    cache_keys = draw_cache_keys(jax.random.fold_in(key_of[9], 71), 0)
    cache_values = bell_draw(key_of[7], (BATCH, CTX, KVH * HD), 1.0, 6.0, ((0, 64), (2, 8)))
    lengths = draw_lengths(jax.random.fold_in(key_of[9], 71), 0)
    return {"master": master, "moment_one": moment_one, "moment_two": moment_two, "gradient": gradient, "hidden": hidden, "queries": queries, "cache_keys": cache_keys, "cache_values": cache_values, "lengths": lengths}


beta_one = 0.9
beta_two = 0.999
learning_rate = 0.0001
weight_decay = 0.1
epsilon = 1e-08
correct_one = 0.9999734386011124
correct_two = 0.09520785288629038

def reference(master, moment_one, moment_two, gradient, hidden, queries, cache_keys, cache_values, lengths):
    grads = gradient.astype(jnp.float32)
    new_moment_one = beta_one * moment_one + (1.0 - beta_one) * grads
    new_moment_two = beta_two * moment_two + (1.0 - beta_two) * grads * grads
    update = new_moment_one / correct_one / (jnp.sqrt(new_moment_two / correct_two) + epsilon)
    new_master = master - learning_rate * (update + weight_decay * master)
    weights = new_master.astype(jnp.bfloat16)
    fresh_flat = jnp.dot(hidden.reshape(BATCH * STEPS, D), weights, preferred_element_type=jnp.float32).astype(jnp.bfloat16)
    fresh_heads = fresh_flat.reshape(BATCH, STEPS, KVH, 2, HD)
    group_size = H // KVH

    def one_request(record):
        query_row, key_row, value_row, new_row, length = record
        query_heads = query_row.astype(jnp.float32).reshape(STEPS, KVH, group_size, HD)
        all_keys = jnp.concatenate([key_row.reshape(CTX, KVH, HD), new_row[:, :, 0, :]], axis=0).astype(jnp.float32)
        all_values = jnp.concatenate([value_row.reshape(CTX, KVH, HD), new_row[:, :, 1, :]], axis=0).astype(jnp.float32)
        scores = jnp.einsum('sgjd,cgd->sgjc', query_heads, all_keys) / math.sqrt(HD)
        places = jnp.arange(CTX + STEPS)
        step_index = jnp.arange(STEPS)
        visible = jnp.where(places[None, :] < CTX, places[None, :] < length, places[None, :] - CTX <= step_index[:, None])
        scores = jnp.where(visible[:, None, None, :], scores, jnp.float32(-1e+30))
        peak = lax.optimization_barrier(jnp.max(scores, axis=-1, keepdims=True))
        expo = jnp.exp(scores - peak)
        probs = lax.optimization_barrier((expo / lax.optimization_barrier(jnp.sum(expo, axis=-1, keepdims=True))).astype(jnp.bfloat16))
        mixture = jnp.einsum('sgjc,cgd->sgjd', probs.astype(jnp.float32), all_values)
        return mixture.astype(jnp.bfloat16).reshape(STEPS, H * HD)
    attended = lax.map(one_request, (queries, cache_keys, cache_values, fresh_heads, lengths))
    return (new_master, new_moment_one, new_moment_two, fresh_flat.reshape(BATCH, STEPS, 2 * KVH * HD), attended)
```

```python
import math

import jax
import jax.numpy as jnp
from jax import lax
from jax.experimental import pallas as pl
from jax.experimental.pallas import tpu as pltpu
from jax.sharding import Mesh, PartitionSpec as P

H = 64
KVH = 8
HD = 128
GROUP = H // KVH

beta_one = 0.9
beta_two = 0.999
learning_rate = 0.0001
weight_decay = 0.1
epsilon = 1e-08
correct_one = 0.9999734386011124
correct_two = 0.09520785288629038

AXES = ("zpair", "zlow", "yfar", "x", "ynear", "core")
SIZES = (8, 2, 2, 4, 2, 2)
LEARN = ("zpair", "zlow")
TP = ("yfar", "x")
REP = ("ynear", "core")
ROWS = LEARN + REP

OFFSET = {0: (1, 2), 1: (1, 1), 2: (0, 2), 3: (0, 1), 4: (0, 0), 5: (0, 3), 6: (1, 0), 7: (1, 3)}


def landing(pair, block):
    far, along = OFFSET[(pair - block) % 8]
    return ((block // 4) ^ far) * 4 + (block % 4 + along) % 4


HOPS = [
    ((pair * 2 + low) * 8 + block, (block * 2 + low) * 8 + landing(pair, block))
    for pair in range(8)
    for low in range(2)
    for block in range(8)
]
VMEM = pl.BlockSpec(memory_space=pltpu.VMEM)
SMEM = pl.BlockSpec(memory_space=pltpu.SMEM)
PARAMS = pltpu.CompilerParams(vmem_limit_bytes=32 * 1024 * 1024)


def slots_kernel(x_ref, out_ref):
    x = x_ref[...].astype(jnp.float32)
    rows = jnp.concatenate([x[0], x[1]], axis=0).astype(jnp.bfloat16)
    for low in range(2):
        part = rows[:, 512 * low : 512 * (low + 1)]
        for t in range(8):
            out_ref[low, t] = part


def project_kernel(y_ref, w_ref, out_ref):
    here = lax.axis_index("zpair")
    w = w_ref[...]
    for low in range(2):
        rows = y_ref[low].astype(jnp.float32).reshape(64, 512).astype(jnp.bfloat16)
        part = jnp.dot(rows, w, preferred_element_type=jnp.float32)
        for t in range(8):
            far = (here // 4) ^ (t // 4)
            along = (t % 4 - here % 4 + 4) % 4
            away = jnp.where(
                far == 0,
                jnp.where(along == 0, 4, jnp.where(along == 1, 3, jnp.where(along == 2, 2, 5))),
                jnp.where(along == 0, 6, jnp.where(along == 1, 1, jnp.where(along == 2, 0, 7))),
            )
            pair = (here + away) % 8
            out_ref[pair, low] = part[8 * t : 8 * t + 8]


def cache_kernel(lengths_ref, q_ref, k_ref, v_ref, heads_ref, acc_ref, peak_ref, total_ref):
    q = q_ref[...].astype(jnp.float32)
    q = jnp.concatenate([q[0], q[1]], axis=0)
    heads = jnp.concatenate([q[:, HD * j : HD * (j + 1)] for j in range(GROUP)], axis=0)
    heads = heads.astype(jnp.bfloat16)
    heads_ref[...] = heads
    context = k_ref.shape[1]
    contract = (((1,), (1,)), ((), ()))
    scores = [
        lax.dot_general(heads, k_ref[b], contract, preferred_element_type=jnp.float32)
        for b in range(2)
    ]
    request = lax.broadcasted_iota(jnp.int32, (64, 1), 0) // 4 % 2
    limit = jnp.where(request == 0, lengths_ref[0], lengths_ref[1])
    slot = lax.broadcasted_iota(jnp.int32, (64, context), 1)
    score = jnp.where(request == 0, scores[0], scores[1]) * (1.0 / math.sqrt(HD))
    score = jnp.where(slot < limit, score, jnp.float32(-1e30))
    peak = jnp.max(score, axis=1, keepdims=True)
    expo = jnp.exp(score - peak)
    total = jnp.sum(expo, axis=1, keepdims=True)
    probs = expo.astype(jnp.bfloat16)
    mixed = [
        jnp.dot(probs, v_ref[b], preferred_element_type=jnp.float32) for b in range(2)
    ]
    acc_ref[...] = jnp.where(request == 0, mixed[0], mixed[1])
    peak_ref[...] = jnp.broadcast_to(peak, (64, HD))
    total_ref[...] = jnp.broadcast_to(total, (64, HD))


def finish_kernel(parts_ref, heads_ref, acc_ref, peak_ref, total_ref, fresh_ref, out_ref):
    fresh = jnp.sum(parts_ref[...], axis=0)
    fresh_ref[0] = fresh[:4].astype(jnp.bfloat16)
    fresh_ref[1] = fresh[4:].astype(jnp.bfloat16)
    fresh = fresh.astype(jnp.bfloat16)
    contract = (((1,), (1,)), ((), ()))
    score = lax.dot_general(
        heads_ref[...], fresh[:, :HD], contract, preferred_element_type=jnp.float32
    ) * (1.0 / math.sqrt(HD))
    row = lax.broadcasted_iota(jnp.int32, (64, 8), 0) % 8
    column = lax.broadcasted_iota(jnp.int32, (64, 8), 1)
    seen = (row // 4 == column // 4) & (column % 4 <= row % 4)
    score = jnp.where(seen, score, jnp.float32(-1e30))
    old_peak = peak_ref[...]
    peak = jnp.maximum(old_peak, jnp.max(score, axis=1, keepdims=True))
    keep = jnp.exp(old_peak - peak)
    expo = jnp.exp(score - peak[:, :8])
    total = total_ref[...] * keep + jnp.sum(expo, axis=1, keepdims=True)
    mixed = jnp.dot(expo.astype(jnp.bfloat16), fresh[:, HD:], preferred_element_type=jnp.float32)
    mixed = (acc_ref[...] * keep + mixed) / total
    for j in range(GROUP):
        block = mixed[8 * j : 8 * j + 8]
        out_ref[0, :, HD * j : HD * (j + 1)] = block[:4].astype(jnp.bfloat16)
        out_ref[1, :, HD * j : HD * (j + 1)] = block[4:].astype(jnp.bfloat16)


def shape(sizes, dtype):
    return jax.ShapeDtypeStruct(sizes, dtype)


def local(
    master, moment_one, moment_two, gradient, hidden, queries, cache_keys, cache_values, lengths
):
    f32, bf16 = jnp.float32, jnp.bfloat16
    moved = lax.ppermute(hidden, LEARN + TP, HOPS)

    grads = gradient.astype(f32)
    new_moment_one = beta_one * moment_one + (1.0 - beta_one) * grads
    new_moment_two = beta_two * moment_two + (1.0 - beta_two) * grads * grads
    update = new_moment_one / correct_one / (jnp.sqrt(new_moment_two / correct_two) + epsilon)
    new_master = master - learning_rate * (update + weight_decay * master)
    weights = lax.all_gather(new_master.astype(bf16), REP, axis=0, tiled=True)
    moved, weights = lax.optimization_barrier((moved, weights))

    slots = pl.pallas_call(
        slots_kernel,
        out_shape=shape((2, 8, 8, 512), bf16),
        in_specs=[VMEM],
        out_specs=VMEM,
        compiler_params=PARAMS,
        name="slots",
    )(moved)
    tokens = lax.all_to_all(slots.reshape(16, 8, 512), ("zlow",) + TP, 0, 0)
    parts = pl.pallas_call(
        project_kernel,
        out_shape=shape((8, 2, 8, 256), f32),
        in_specs=[VMEM, VMEM],
        out_specs=VMEM,
        compiler_params=PARAMS,
        name="project",
    )(tokens.reshape(2, 8, 8, 512), weights)
    parts, queries = lax.optimization_barrier((parts, queries))
    parts = lax.all_to_all(parts.reshape(16, 8, 256), LEARN, 0, 0)
    cached = pl.pallas_call(
        cache_kernel,
        out_shape=[shape((64, HD), bf16)] + [shape((64, HD), f32)] * 3,
        in_specs=[SMEM] + [VMEM] * 3,
        out_specs=[VMEM] * 4,
        compiler_params=PARAMS,
        cost_estimate=pl.CostEstimate(
            flops=4 * 64 * 4096 * 128, bytes_accessed=1 << 22, transcendentals=64 * 2048
        ),
        name="cache",
    )(lengths, queries, cache_keys, cache_values)
    fresh_kv, attended = pl.pallas_call(
        finish_kernel,
        out_shape=[shape((2, 4, 256), bf16), shape((2, 4, 1024), bf16)],
        in_specs=[VMEM] * 5,
        out_specs=[VMEM] * 2,
        compiler_params=PARAMS,
        name="finish",
    )(parts, *cached)
    return new_master, new_moment_one, new_moment_two, fresh_kv, attended


def solution(mesh):
    fine = Mesh(mesh.devices.reshape(SIZES), AXES)
    square = P(ROWS, TP)
    rows = P(ROWS, None, TP)
    return jax.shard_map(
        local,
        mesh=fine,
        in_specs=(square, square, square, square, rows, rows, rows, rows, P(ROWS)),
        out_specs=(square, square, square, rows, rows),
        check_vma=False,
    )
```

```python
import math

import jax
import jax.numpy as jnp
from jax import lax
from jax.experimental import pallas as pl
from jax.experimental.pallas import tpu as pltpu
from jax.sharding import Mesh, PartitionSpec as P

H = 64
KVH = 8
HD = 128
GROUP = H // KVH

beta_one = 0.9
beta_two = 0.999
learning_rate = 0.0001
weight_decay = 0.1
epsilon = 1e-08
correct_one = 0.9999734386011124
correct_two = 0.09520785288629038

AXES = ("zpair", "zlow", "yfar", "x", "ynear", "core")
SIZES = (8, 2, 2, 4, 2, 2)
LEARN = ("zpair", "zlow")
TP = ("yfar", "x")
REP = ("ynear", "core")
ROWS = LEARN + REP

OFFSET = {0: (1, 2), 1: (1, 1), 2: (0, 2), 3: (0, 1), 4: (0, 0), 5: (0, 3), 6: (1, 0), 7: (1, 3)}


def landing(pair, block):
    far, along = OFFSET[(pair - block) % 8]
    return ((block // 4) ^ far) * 4 + (block % 4 + along) % 4


HOPS = [
    ((pair * 2 + low) * 8 + block, (block * 2 + low) * 8 + landing(pair, block))
    for pair in range(8)
    for low in range(2)
    for block in range(8)
]
BLOCKS = [(i + 4) % 8 for i in range(8)]
PAIRS = [(i + 4) % 8 for i in range(8)]
VMEM = pl.BlockSpec(memory_space=pltpu.VMEM)
SMEM = pl.BlockSpec(memory_space=pltpu.SMEM)
PARAMS = pltpu.CompilerParams(vmem_limit_bytes=32 * 1024 * 1024)


def slots_kernel(x_ref, out_ref):
    x = x_ref[...].astype(jnp.float32)
    rows = jnp.concatenate([x[0], x[1]], axis=0).astype(jnp.bfloat16)
    for t in range(8):
        out_ref[t] = rows


def project_kernel(y_ref, own_ref, other_ref, out_ref):
    here = lax.axis_index("zpair")
    low = lax.axis_index("zlow")
    rows = y_ref[...].astype(jnp.float32).reshape(64, 1024)
    first, second = rows[:, :512], rows[:, 512:]
    mine = jnp.where(low == 0, first, second).astype(jnp.bfloat16)
    theirs = jnp.where(low == 0, second, first).astype(jnp.bfloat16)
    part = jnp.dot(mine, own_ref[...], preferred_element_type=jnp.float32)
    part = part + jnp.dot(theirs, other_ref[...], preferred_element_type=jnp.float32)
    for i, t in enumerate(BLOCKS):
        far = (here // 4) ^ (t // 4)
        along = (t % 4 - here % 4 + 4) % 4
        away = jnp.where(
            far == 0,
            jnp.where(along == 0, 4, jnp.where(along == 1, 3, jnp.where(along == 2, 2, 5))),
            jnp.where(along == 0, 6, jnp.where(along == 1, 1, jnp.where(along == 2, 0, 7))),
        )
        out_ref[(here + away + 8 - PAIRS[0]) % 8] = part[8 * i : 8 * i + 8]


def cache_kernel(lengths_ref, q_ref, k_ref, v_ref, heads_ref, acc_ref, peak_ref, total_ref):
    q = q_ref[...].astype(jnp.float32)
    q = jnp.concatenate([q[0], q[1]], axis=0)
    heads = jnp.concatenate([q[:, HD * j : HD * (j + 1)] for j in range(GROUP)], axis=0)
    heads = heads.astype(jnp.bfloat16)
    heads_ref[...] = heads
    context = k_ref.shape[1]
    contract = (((1,), (1,)), ((), ()))
    scores = [
        lax.dot_general(heads, k_ref[b], contract, preferred_element_type=jnp.float32)
        for b in range(2)
    ]
    request = lax.broadcasted_iota(jnp.int32, (64, 1), 0) // 4 % 2
    limit = jnp.where(request == 0, lengths_ref[0], lengths_ref[1])
    slot = lax.broadcasted_iota(jnp.int32, (64, context), 1)
    score = jnp.where(request == 0, scores[0], scores[1]) * (1.0 / math.sqrt(HD))
    score = jnp.where(slot < limit, score, jnp.float32(-1e30))
    peak = jnp.max(score, axis=1, keepdims=True)
    expo = jnp.exp(score - peak)
    total = jnp.sum(expo, axis=1, keepdims=True)
    probs = expo.astype(jnp.bfloat16)
    mixed = [
        jnp.dot(probs, v_ref[b], preferred_element_type=jnp.float32) for b in range(2)
    ]
    acc_ref[...] = jnp.where(request == 0, mixed[0], mixed[1])
    peak_ref[...] = jnp.broadcast_to(peak, (64, HD))
    total_ref[...] = jnp.broadcast_to(total, (64, HD))


def finish_kernel(parts_ref, heads_ref, acc_ref, peak_ref, total_ref, fresh_ref, out_ref):
    fresh = jnp.sum(parts_ref[...], axis=0)
    fresh_ref[0] = fresh[:4].astype(jnp.bfloat16)
    fresh_ref[1] = fresh[4:].astype(jnp.bfloat16)
    fresh = fresh.astype(jnp.bfloat16)
    contract = (((1,), (1,)), ((), ()))
    score = lax.dot_general(
        heads_ref[...], fresh[:, :HD], contract, preferred_element_type=jnp.float32
    ) * (1.0 / math.sqrt(HD))
    row = lax.broadcasted_iota(jnp.int32, (64, 8), 0) % 8
    column = lax.broadcasted_iota(jnp.int32, (64, 8), 1)
    seen = (row // 4 == column // 4) & (column % 4 <= row % 4)
    score = jnp.where(seen, score, jnp.float32(-1e30))
    old_peak = peak_ref[...]
    peak = jnp.maximum(old_peak, jnp.max(score, axis=1, keepdims=True))
    keep = jnp.exp(old_peak - peak)
    expo = jnp.exp(score - peak[:, :8])
    total = total_ref[...] * keep + jnp.sum(expo, axis=1, keepdims=True)
    mixed = jnp.dot(expo.astype(jnp.bfloat16), fresh[:, HD:], preferred_element_type=jnp.float32)
    mixed = (acc_ref[...] * keep + mixed) / total
    for j in range(GROUP):
        block = mixed[8 * j : 8 * j + 8]
        out_ref[0, :, HD * j : HD * (j + 1)] = block[:4].astype(jnp.bfloat16)
        out_ref[1, :, HD * j : HD * (j + 1)] = block[4:].astype(jnp.bfloat16)


def shape(sizes, dtype):
    return jax.ShapeDtypeStruct(sizes, dtype)


def local(
    master, moment_one, moment_two, gradient, hidden, queries, cache_keys, cache_values, lengths
):
    f32, bf16 = jnp.float32, jnp.bfloat16
    moved = lax.ppermute(hidden, LEARN + TP, HOPS)

    def adamw(master, moment_one, moment_two, gradient):
        grads = gradient.astype(f32)
        new_moment_one = beta_one * moment_one + (1.0 - beta_one) * grads
        new_moment_two = beta_two * moment_two + (1.0 - beta_two) * grads * grads
        update = new_moment_one / correct_one / (jnp.sqrt(new_moment_two / correct_two) + epsilon)
        new_master = master - learning_rate * (update + weight_decay * master)
        return new_master, new_moment_one, new_moment_two

    weights = adamw(master, moment_one, moment_two, gradient)[0].astype(bf16)
    weights = lax.all_gather(weights, REP, axis=0, tiled=True)
    moved, weights = lax.optimization_barrier((moved, weights))
    others = lax.ppermute(weights, "zlow", [(0, 1), (1, 0)])
    slots = pl.pallas_call(
        slots_kernel,
        out_shape=shape((8, 8, 1024), bf16),
        in_specs=[VMEM],
        out_specs=VMEM,
        compiler_params=PARAMS,
        name="slots",
    )(moved)
    tokens = lax.all_to_all(slots, TP, 0, 0, axis_index_groups=[BLOCKS])
    parts = pl.pallas_call(
        project_kernel,
        out_shape=shape((8, 8, 256), f32),
        in_specs=[VMEM] * 3,
        out_specs=VMEM,
        compiler_params=PARAMS,
        name="project",
    )(tokens, weights, others)
    parts, queries, *state = lax.optimization_barrier(
        (parts, queries, master, moment_one, moment_two, gradient)
    )
    new_master, new_moment_one, new_moment_two = adamw(*state)
    parts = lax.all_to_all(parts, "zpair", 0, 0, axis_index_groups=[PAIRS])
    cached = pl.pallas_call(
        cache_kernel,
        out_shape=[shape((64, HD), bf16)] + [shape((64, HD), f32)] * 3,
        in_specs=[SMEM] + [VMEM] * 3,
        out_specs=[VMEM] * 4,
        compiler_params=PARAMS,
        cost_estimate=pl.CostEstimate(
            flops=4 * 64 * 4096 * 128, bytes_accessed=1 << 22, transcendentals=64 * 2048
        ),
        name="cache",
    )(lengths, queries, cache_keys, cache_values)
    fresh_kv, attended = pl.pallas_call(
        finish_kernel,
        out_shape=[shape((2, 4, 256), bf16), shape((2, 4, 1024), bf16)],
        in_specs=[VMEM] * 5,
        out_specs=[VMEM] * 2,
        compiler_params=PARAMS,
        name="finish",
    )(parts, *cached)
    return new_master, new_moment_one, new_moment_two, fresh_kv, attended


def solution(mesh):
    fine = Mesh(mesh.devices.reshape(SIZES), AXES)
    square = P(ROWS, TP)
    rows = P(ROWS, None, TP)
    return jax.shard_map(
        local,
        mesh=fine,
        in_specs=(square, square, square, square, rows, rows, rows, rows, P(ROWS)),
        out_specs=(square, square, square, rows, rows),
        check_vma=False,
    )
```

```python
import math

import jax
import jax.numpy as jnp
from jax import lax
from jax.experimental import pallas as pl
from jax.experimental.pallas import tpu as pltpu
from jax.sharding import Mesh, PartitionSpec as P

H = 64
KVH = 8
HD = 128
GROUP = H // KVH

beta_one = 0.9
beta_two = 0.999
learning_rate = 0.0001
weight_decay = 0.1
epsilon = 1e-08
correct_one = 0.9999734386011124
correct_two = 0.09520785288629038

AXES = ("zpair", "zlow", "yfar", "x", "ynear", "core")
SIZES = (8, 2, 2, 4, 2, 2)
LEARN = ("zpair", "zlow")
TP = ("yfar", "x")
REP = ("ynear", "core")
ROWS = LEARN + REP

OFFSET = {0: (1, 2), 1: (1, 1), 2: (0, 2), 3: (0, 1), 4: (0, 0), 5: (0, 3), 6: (1, 0), 7: (1, 3)}


def landing(pair, block):
    far, along = OFFSET[(pair - block) % 8]
    return ((block // 4) ^ far) * 4 + (block % 4 + along) % 4


HOPS = [
    ((pair * 2 + low) * 8 + block, (block * 2 + low) * 8 + landing(pair, block))
    for pair in range(8)
    for low in range(2)
    for block in range(8)
]
BLOCKS = [(i + 4) % 8 for i in range(8)]
PAIRS = [(i + 4) % 8 for i in range(8)]
VMEM = pl.BlockSpec(memory_space=pltpu.VMEM)
SMEM = pl.BlockSpec(memory_space=pltpu.SMEM)
PARAMS = pltpu.CompilerParams(vmem_limit_bytes=32 * 1024 * 1024)


def mask_kernel(out_ref):
    row = lax.broadcasted_iota(jnp.int32, (64, 8), 0) % 8
    column = lax.broadcasted_iota(jnp.int32, (64, 8), 1)
    seen = (row // 4 == column // 4) & (column % 4 <= row % 4)
    out_ref[...] = jnp.where(seen, jnp.float32(0), jnp.float32(-1e30))


def slots_kernel(x_ref, out_ref):
    x = x_ref[...].astype(jnp.float32)
    rows = jnp.concatenate([x[0], x[1]], axis=0).astype(jnp.bfloat16)
    for t in range(8):
        out_ref[t] = rows


def project_kernel(y_ref, own_ref, other_ref, out_ref):
    here = lax.axis_index("zpair")
    low = lax.axis_index("zlow")
    rows = y_ref[...].astype(jnp.float32).reshape(64, 1024)
    first, second = rows[:, :512], rows[:, 512:]
    mine = jnp.where(low == 0, first, second).astype(jnp.bfloat16)
    theirs = jnp.where(low == 0, second, first).astype(jnp.bfloat16)
    part = jnp.dot(mine, own_ref[...], preferred_element_type=jnp.float32)
    part = part + jnp.dot(theirs, other_ref[...], preferred_element_type=jnp.float32)
    for i, t in enumerate(BLOCKS):
        far = (here // 4) ^ (t // 4)
        along = (t % 4 - here % 4 + 4) % 4
        away = jnp.where(
            far == 0,
            jnp.where(along == 0, 4, jnp.where(along == 1, 3, jnp.where(along == 2, 2, 5))),
            jnp.where(along == 0, 6, jnp.where(along == 1, 1, jnp.where(along == 2, 0, 7))),
        )
        out_ref[(here + away + 8 - PAIRS[0]) % 8] = part[8 * i : 8 * i + 8]


def cache_kernel(lengths_ref, q_ref, k_ref, v_ref, heads_ref, acc_ref, peak_ref, total_ref):
    q = q_ref[...].astype(jnp.float32)
    q = jnp.concatenate([q[0], q[1]], axis=0)
    heads = jnp.concatenate([q[:, HD * j : HD * (j + 1)] for j in range(GROUP)], axis=0)
    heads = heads.astype(jnp.bfloat16)
    heads_ref[...] = heads
    context = k_ref.shape[1]
    contract = (((1,), (1,)), ((), ()))
    scores = [
        lax.dot_general(heads, k_ref[b], contract, preferred_element_type=jnp.float32)
        for b in range(2)
    ]
    request = lax.broadcasted_iota(jnp.int32, (64, 1), 0) // 4 % 2
    limit = jnp.where(request == 0, lengths_ref[0], lengths_ref[1])
    slot = lax.broadcasted_iota(jnp.int32, (64, context), 1)
    score = jnp.where(request == 0, scores[0], scores[1]) * (1.0 / math.sqrt(HD))
    score = jnp.where(slot < limit, score, jnp.float32(-1e30))
    peak = jnp.max(score, axis=1, keepdims=True)
    expo = jnp.exp(score - peak)
    total = jnp.sum(expo, axis=1, keepdims=True)
    probs = expo.astype(jnp.bfloat16)
    mixed = [
        jnp.dot(probs, v_ref[b], preferred_element_type=jnp.float32) for b in range(2)
    ]
    acc_ref[...] = jnp.where(request == 0, mixed[0], mixed[1])
    peak_ref[...] = jnp.broadcast_to(peak, (64, HD))
    total_ref[...] = jnp.broadcast_to(total, (64, HD))


def finish_kernel(parts_ref, mask_ref, heads_ref, acc_ref, peak_ref, total_ref, fresh_ref, out_ref):
    fresh = jnp.sum(parts_ref[...], axis=0)
    fresh_ref[0] = fresh[:4].astype(jnp.bfloat16)
    fresh_ref[1] = fresh[4:].astype(jnp.bfloat16)
    fresh = fresh.astype(jnp.bfloat16)
    contract = (((1,), (1,)), ((), ()))
    score = lax.dot_general(
        heads_ref[...], fresh[:, :HD], contract, preferred_element_type=jnp.float32
    ) * (1.0 / math.sqrt(HD))
    score = jnp.where(mask_ref[...] == 0, score, jnp.float32(-1e30))
    old_peak = peak_ref[...]
    peak = jnp.maximum(old_peak, jnp.max(score, axis=1, keepdims=True))
    keep = jnp.exp(old_peak - peak)
    expo = jnp.exp(score - peak[:, :8])
    total = total_ref[...] * keep + jnp.sum(expo, axis=1, keepdims=True)
    mixed = jnp.dot(expo.astype(jnp.bfloat16), fresh[:, HD:], preferred_element_type=jnp.float32)
    mixed = (acc_ref[...] * keep + mixed) / total
    for j in range(GROUP):
        block = mixed[8 * j : 8 * j + 8]
        out_ref[0, :, HD * j : HD * (j + 1)] = block[:4].astype(jnp.bfloat16)
        out_ref[1, :, HD * j : HD * (j + 1)] = block[4:].astype(jnp.bfloat16)


def shape(sizes, dtype):
    return jax.ShapeDtypeStruct(sizes, dtype)


def local(
    master, moment_one, moment_two, gradient, hidden, queries, cache_keys, cache_values, lengths
):
    f32, bf16 = jnp.float32, jnp.bfloat16
    moved = lax.ppermute(hidden, LEARN + TP, HOPS)

    def adamw(master, moment_one, moment_two, gradient):
        grads = gradient.astype(f32)
        new_moment_one = beta_one * moment_one + (1.0 - beta_one) * grads
        new_moment_two = beta_two * moment_two + (1.0 - beta_two) * grads * grads
        update = new_moment_one / correct_one / (jnp.sqrt(new_moment_two / correct_two) + epsilon)
        new_master = master - learning_rate * (update + weight_decay * master)
        return new_master, new_moment_one, new_moment_two

    mask = pl.pallas_call(
        mask_kernel,
        out_shape=shape((64, 8), f32),
        out_specs=VMEM,
        compiler_params=PARAMS,
        cost_estimate=pl.CostEstimate(
            flops=4 * 64 * 4096 * 128, bytes_accessed=1 << 22, transcendentals=64 * 2048
        ),
        name="mask",
    )()
    state, mask = lax.optimization_barrier(((master, moment_one, moment_two, gradient), mask))
    weights = adamw(*state)[0].astype(bf16)
    weights = lax.all_gather(weights, REP, axis=0, tiled=True)
    moved, weights = lax.optimization_barrier((moved, weights))
    others = lax.ppermute(weights, "zlow", [(0, 1), (1, 0)])
    slots = pl.pallas_call(
        slots_kernel,
        out_shape=shape((8, 8, 1024), bf16),
        in_specs=[VMEM],
        out_specs=VMEM,
        compiler_params=PARAMS,
        name="slots",
    )(moved)
    tokens = lax.all_to_all(slots, TP, 0, 0, axis_index_groups=[BLOCKS])
    parts = pl.pallas_call(
        project_kernel,
        out_shape=shape((8, 8, 256), f32),
        in_specs=[VMEM] * 3,
        out_specs=VMEM,
        compiler_params=PARAMS,
        name="project",
    )(tokens, weights, others)
    parts, queries, *state = lax.optimization_barrier(
        (parts, queries, master, moment_one, moment_two, gradient)
    )
    new_master, new_moment_one, new_moment_two = adamw(*state)
    parts = lax.all_to_all(parts, "zpair", 0, 0, axis_index_groups=[PAIRS])
    cached = pl.pallas_call(
        cache_kernel,
        out_shape=[shape((64, HD), bf16)] + [shape((64, HD), f32)] * 3,
        in_specs=[SMEM] + [VMEM] * 3,
        out_specs=[VMEM] * 4,
        compiler_params=PARAMS,
        cost_estimate=pl.CostEstimate(
            flops=4 * 64 * 4096 * 128, bytes_accessed=1 << 22, transcendentals=64 * 2048
        ),
        name="cache",
    )(lengths, queries, cache_keys, cache_values)
    fresh_kv, attended = pl.pallas_call(
        finish_kernel,
        out_shape=[shape((2, 4, 256), bf16), shape((2, 4, 1024), bf16)],
        in_specs=[VMEM] * 6,
        out_specs=[VMEM] * 2,
        compiler_params=PARAMS,
        name="finish",
    )(parts, mask, *cached)
    return new_master, new_moment_one, new_moment_two, fresh_kv, attended


def solution(mesh):
    fine = Mesh(mesh.devices.reshape(SIZES), AXES)
    square = P(ROWS, TP)
    rows = P(ROWS, None, TP)
    return jax.shard_map(
        local,
        mesh=fine,
        in_specs=(square, square, square, square, rows, rows, rows, rows, P(ROWS)),
        out_specs=(square, square, square, rows, rows),
        check_vma=False,
    )
```

```python
import math

import jax
import jax.numpy as jnp
from jax import lax
from jax.experimental import pallas as pl
from jax.experimental.pallas import tpu as pltpu
from jax.sharding import Mesh, PartitionSpec as P

H = 64
KVH = 8
HD = 128
GROUP = H // KVH

beta_one = 0.9
beta_two = 0.999
learning_rate = 0.0001
weight_decay = 0.1
epsilon = 1e-08
correct_one = 0.9999734386011124
correct_two = 0.09520785288629038

AXES = ("zpair", "zlow", "yfar", "x", "ynear", "core")
SIZES = (8, 2, 2, 4, 2, 2)
LEARN = ("zpair", "zlow")
TP = ("yfar", "x")
REP = ("ynear", "core")
ROWS = LEARN + REP

OFFSET = {0: (1, 2), 1: (1, 1), 2: (0, 2), 3: (0, 1), 4: (0, 0), 5: (0, 3), 6: (1, 0), 7: (1, 3)}


def landing(pair, block):
    far, along = OFFSET[(pair - block) % 8]
    return ((block // 4) ^ far) * 4 + (block % 4 + along) % 4


HOPS = [
    ((pair * 2 + low) * 8 + block, (block * 2 + low) * 8 + landing(pair, block))
    for pair in range(8)
    for low in range(2)
    for block in range(8)
]
ROOTS = (4, 4, 5, 7, 7, 5, 7, 7)
PLANES = [[8 * plane + (i + root) % 8 for i in range(8)] for plane, root in enumerate(ROOTS)]
PAIRS = [(i + 4) % 8 for i in range(8)]
VMEM = pl.BlockSpec(memory_space=pltpu.VMEM)
SMEM = pl.BlockSpec(memory_space=pltpu.SMEM)
PARAMS = pltpu.CompilerParams(vmem_limit_bytes=32 * 1024 * 1024)


def mask_kernel(out_ref):
    row = lax.broadcasted_iota(jnp.int32, (64, 8), 0) % 8
    column = lax.broadcasted_iota(jnp.int32, (64, 8), 1)
    seen = (row // 4 == column // 4) & (column % 4 <= row % 4)
    out_ref[...] = jnp.where(seen, jnp.float32(0), jnp.float32(-1e30))


def slots_kernel(x_ref, out_ref):
    x = x_ref[...].astype(jnp.float32)
    rows = jnp.concatenate([x[0], x[1]], axis=0).astype(jnp.bfloat16)
    for t in range(8):
        out_ref[t] = rows


def project_kernel(y_ref, own_ref, other_ref, out_ref):
    here = lax.axis_index("zpair")
    low = lax.axis_index("zlow")
    rows = y_ref[...].astype(jnp.float32).reshape(64, 1024)
    left, right = rows[:, :512], rows[:, 512:]
    mine = jnp.where(low == 0, left, right).astype(jnp.bfloat16)
    theirs = jnp.where(low == 0, right, left).astype(jnp.bfloat16)
    part = jnp.dot(mine, own_ref[...], preferred_element_type=jnp.float32)
    part = part + jnp.dot(theirs, other_ref[...], preferred_element_type=jnp.float32)
    first = jnp.int32(ROOTS[0])
    for plane in range(1, 8):
        first = jnp.where(here == plane, ROOTS[plane], first)
    for i in range(8):
        t = (i + first) % 8
        far = (here // 4) ^ (t // 4)
        along = (t % 4 - here % 4 + 4) % 4
        away = jnp.where(
            far == 0,
            jnp.where(along == 0, 4, jnp.where(along == 1, 3, jnp.where(along == 2, 2, 5))),
            jnp.where(along == 0, 6, jnp.where(along == 1, 1, jnp.where(along == 2, 0, 7))),
        )
        out_ref[(here + away + 8 - PAIRS[0]) % 8] = part[8 * i : 8 * i + 8]


def cache_kernel(lengths_ref, q_ref, k_ref, v_ref, heads_ref, acc_ref, peak_ref, total_ref):
    q = q_ref[...].astype(jnp.float32)
    q = jnp.concatenate([q[0], q[1]], axis=0)
    heads = jnp.concatenate([q[:, HD * j : HD * (j + 1)] for j in range(GROUP)], axis=0)
    heads = heads.astype(jnp.bfloat16)
    heads_ref[...] = heads
    context = k_ref.shape[1]
    contract = (((1,), (1,)), ((), ()))
    scores = [
        lax.dot_general(heads, k_ref[b], contract, preferred_element_type=jnp.float32)
        for b in range(2)
    ]
    request = lax.broadcasted_iota(jnp.int32, (64, 1), 0) // 4 % 2
    limit = jnp.where(request == 0, lengths_ref[0], lengths_ref[1])
    slot = lax.broadcasted_iota(jnp.int32, (64, context), 1)
    score = jnp.where(request == 0, scores[0], scores[1]) * (1.0 / math.sqrt(HD))
    score = jnp.where(slot < limit, score, jnp.float32(-1e30))
    peak = jnp.max(score, axis=1, keepdims=True)
    expo = jnp.exp(score - peak)
    total = jnp.sum(expo, axis=1, keepdims=True)
    probs = expo.astype(jnp.bfloat16)
    mixed = [
        jnp.dot(probs, v_ref[b], preferred_element_type=jnp.float32) for b in range(2)
    ]
    acc_ref[...] = jnp.where(request == 0, mixed[0], mixed[1])
    peak_ref[...] = jnp.broadcast_to(peak, (64, HD))
    total_ref[...] = jnp.broadcast_to(total, (64, HD))


def finish_kernel(parts_ref, mask_ref, heads_ref, acc_ref, peak_ref, total_ref, fresh_ref, out_ref):
    fresh = jnp.sum(parts_ref[...], axis=0)
    fresh_ref[0] = fresh[:4].astype(jnp.bfloat16)
    fresh_ref[1] = fresh[4:].astype(jnp.bfloat16)
    fresh = fresh.astype(jnp.bfloat16)
    contract = (((1,), (1,)), ((), ()))
    score = lax.dot_general(
        heads_ref[...], fresh[:, :HD], contract, preferred_element_type=jnp.float32
    ) * (1.0 / math.sqrt(HD))
    score = jnp.where(mask_ref[...] == 0, score, jnp.float32(-1e30))
    old_peak = peak_ref[...]
    peak = jnp.maximum(old_peak, jnp.max(score, axis=1, keepdims=True))
    keep = jnp.exp(old_peak - peak)
    expo = jnp.exp(score - peak[:, :8])
    total = total_ref[...] * keep + jnp.sum(expo, axis=1, keepdims=True)
    mixed = jnp.dot(expo.astype(jnp.bfloat16), fresh[:, HD:], preferred_element_type=jnp.float32)
    mixed = (acc_ref[...] * keep + mixed) / total
    for j in range(GROUP):
        block = mixed[8 * j : 8 * j + 8]
        out_ref[0, :, HD * j : HD * (j + 1)] = block[:4].astype(jnp.bfloat16)
        out_ref[1, :, HD * j : HD * (j + 1)] = block[4:].astype(jnp.bfloat16)


def shape(sizes, dtype):
    return jax.ShapeDtypeStruct(sizes, dtype)


def local(
    master, moment_one, moment_two, gradient, hidden, queries, cache_keys, cache_values, lengths
):
    f32, bf16 = jnp.float32, jnp.bfloat16
    moved = lax.ppermute(hidden, LEARN + TP, HOPS)

    def adamw(master, moment_one, moment_two, gradient):
        grads = gradient.astype(f32)
        new_moment_one = beta_one * moment_one + (1.0 - beta_one) * grads
        new_moment_two = beta_two * moment_two + (1.0 - beta_two) * grads * grads
        update = new_moment_one / correct_one / (jnp.sqrt(new_moment_two / correct_two) + epsilon)
        new_master = master - learning_rate * (update + weight_decay * master)
        return new_master, new_moment_one, new_moment_two

    mask = pl.pallas_call(
        mask_kernel,
        out_shape=shape((64, 8), f32),
        out_specs=VMEM,
        compiler_params=PARAMS,
        cost_estimate=pl.CostEstimate(
            flops=4 * 64 * 4096 * 128, bytes_accessed=1 << 22, transcendentals=64 * 2048
        ),
        name="mask",
    )()
    state, mask = lax.optimization_barrier(((master, moment_one, moment_two, gradient), mask))
    weights = adamw(*state)[0].astype(bf16)
    weights = lax.all_gather(weights, REP, axis=0, tiled=True)
    moved, weights = lax.optimization_barrier((moved, weights))
    others = lax.ppermute(weights, "zlow", [(0, 1), (1, 0)])
    slots = pl.pallas_call(
        slots_kernel,
        out_shape=shape((8, 8, 1024), bf16),
        in_specs=[VMEM],
        out_specs=VMEM,
        compiler_params=PARAMS,
        name="slots",
    )(moved)
    tokens = lax.all_to_all(slots, ("zpair",) + TP, 0, 0, axis_index_groups=PLANES)
    parts = pl.pallas_call(
        project_kernel,
        out_shape=shape((8, 8, 256), f32),
        in_specs=[VMEM] * 3,
        out_specs=VMEM,
        compiler_params=PARAMS,
        name="project",
    )(tokens, weights, others)
    parts, queries, *state = lax.optimization_barrier(
        (parts, queries, master, moment_one, moment_two, gradient)
    )
    new_master, new_moment_one, new_moment_two = adamw(*state)
    parts = lax.all_to_all(parts, "zpair", 0, 0, axis_index_groups=[PAIRS])
    cached = pl.pallas_call(
        cache_kernel,
        out_shape=[shape((64, HD), bf16)] + [shape((64, HD), f32)] * 3,
        in_specs=[SMEM] + [VMEM] * 3,
        out_specs=[VMEM] * 4,
        compiler_params=PARAMS,
        cost_estimate=pl.CostEstimate(
            flops=4 * 64 * 4096 * 128, bytes_accessed=1 << 22, transcendentals=64 * 2048
        ),
        name="cache",
    )(lengths, queries, cache_keys, cache_values)
    fresh_kv, attended = pl.pallas_call(
        finish_kernel,
        out_shape=[shape((2, 4, 256), bf16), shape((2, 4, 1024), bf16)],
        in_specs=[VMEM] * 6,
        out_specs=[VMEM] * 2,
        compiler_params=PARAMS,
        name="finish",
    )(parts, mask, *cached)
    return new_master, new_moment_one, new_moment_two, fresh_kv, attended


def solution(mesh):
    fine = Mesh(mesh.devices.reshape(SIZES), AXES)
    square = P(ROWS, TP)
    rows = P(ROWS, None, TP)
    return jax.shard_map(
        local,
        mesh=fine,
        in_specs=(square, square, square, square, rows, rows, rows, rows, P(ROWS)),
        out_specs=(square, square, square, rows, rows),
        check_vma=False,
    )
```

```python
import math

import jax
import jax.numpy as jnp
from jax import lax
from jax.experimental import pallas as pl
from jax.experimental.pallas import tpu as pltpu
from jax.sharding import Mesh, PartitionSpec as P

H = 64
KVH = 8
HD = 128
GROUP = H // KVH

beta_one = 0.9
beta_two = 0.999
learning_rate = 0.0001
weight_decay = 0.1
epsilon = 1e-08
correct_one = 0.9999734386011124
correct_two = 0.09520785288629038

AXES = ("zpair", "zlow", "yfar", "x", "ynear", "core")
SIZES = (8, 2, 2, 4, 2, 2)
LEARN = ("zpair", "zlow")
TP = ("yfar", "x")
REP = ("ynear", "core")
ROWS = LEARN + REP

OFFSET = {0: (1, 2), 1: (1, 1), 2: (0, 2), 3: (0, 1), 4: (0, 0), 5: (0, 3), 6: (1, 0), 7: (1, 3)}


def landing(pair, block):
    far, along = OFFSET[(pair - block) % 8]
    return ((block // 4) ^ far) * 4 + (block % 4 + along) % 4


HOPS = [
    ((pair * 2 + low) * 8 + block, (block * 2 + low) * 8 + landing(pair, block))
    for pair in range(8)
    for low in range(2)
    for block in range(8)
]
BLOCKS = [4, 0, 5, 1, 6, 2, 7, 3]
PAIRS = [(i + 4) % 8 for i in range(8)]
VMEM = pl.BlockSpec(memory_space=pltpu.VMEM)
SMEM = pl.BlockSpec(memory_space=pltpu.SMEM)
PARAMS = pltpu.CompilerParams(vmem_limit_bytes=32 * 1024 * 1024)


def mask_kernel(out_ref):
    row = lax.broadcasted_iota(jnp.int32, (64, 8), 0) % 8
    column = lax.broadcasted_iota(jnp.int32, (64, 8), 1)
    seen = (row // 4 == column // 4) & (column % 4 <= row % 4)
    out_ref[...] = jnp.where(seen, jnp.float32(0), jnp.float32(-1e30))


def slots_kernel(x_ref, out_ref):
    x = x_ref[...].astype(jnp.float32)
    rows = jnp.concatenate([x[0], x[1]], axis=0).astype(jnp.bfloat16)
    for t in range(8):
        out_ref[t] = rows


def project_kernel(y_ref, own_ref, other_ref, out_ref):
    here = lax.axis_index("zpair")
    low = lax.axis_index("zlow")
    rows = y_ref[...].astype(jnp.float32).reshape(64, 1024)
    first, second = rows[:, :512], rows[:, 512:]
    mine = jnp.where(low == 0, first, second).astype(jnp.bfloat16)
    theirs = jnp.where(low == 0, second, first).astype(jnp.bfloat16)
    part = jnp.dot(mine, own_ref[...], preferred_element_type=jnp.float32)
    part = part + jnp.dot(theirs, other_ref[...], preferred_element_type=jnp.float32)
    for i, t in enumerate(BLOCKS):
        far = (here // 4) ^ (t // 4)
        along = (t % 4 - here % 4 + 4) % 4
        away = jnp.where(
            far == 0,
            jnp.where(along == 0, 4, jnp.where(along == 1, 3, jnp.where(along == 2, 2, 5))),
            jnp.where(along == 0, 6, jnp.where(along == 1, 1, jnp.where(along == 2, 0, 7))),
        )
        out_ref[(here + away + 8 - PAIRS[0]) % 8] = part[8 * i : 8 * i + 8]


def cache_kernel(lengths_ref, q_ref, k_ref, v_ref, heads_ref, acc_ref, peak_ref, total_ref):
    q = q_ref[...].astype(jnp.float32)
    q = jnp.concatenate([q[0], q[1]], axis=0)
    heads = jnp.concatenate([q[:, HD * j : HD * (j + 1)] for j in range(GROUP)], axis=0)
    heads = heads.astype(jnp.bfloat16)
    heads_ref[...] = heads
    context = k_ref.shape[1]
    contract = (((1,), (1,)), ((), ()))
    scores = [
        lax.dot_general(heads, k_ref[b], contract, preferred_element_type=jnp.float32)
        for b in range(2)
    ]
    request = lax.broadcasted_iota(jnp.int32, (64, 1), 0) // 4 % 2
    limit = jnp.where(request == 0, lengths_ref[0], lengths_ref[1])
    slot = lax.broadcasted_iota(jnp.int32, (64, context), 1)
    score = jnp.where(request == 0, scores[0], scores[1]) * (1.0 / math.sqrt(HD))
    score = jnp.where(slot < limit, score, jnp.float32(-1e30))
    peak = jnp.max(score, axis=1, keepdims=True)
    expo = jnp.exp(score - peak)
    total = jnp.sum(expo, axis=1, keepdims=True)
    probs = expo.astype(jnp.bfloat16)
    mixed = [
        jnp.dot(probs, v_ref[b], preferred_element_type=jnp.float32) for b in range(2)
    ]
    acc_ref[...] = jnp.where(request == 0, mixed[0], mixed[1])
    peak_ref[...] = jnp.broadcast_to(peak, (64, HD))
    total_ref[...] = jnp.broadcast_to(total, (64, HD))


def finish_kernel(parts_ref, mask_ref, heads_ref, acc_ref, peak_ref, total_ref, fresh_ref, out_ref):
    fresh = jnp.sum(parts_ref[...], axis=0)
    fresh_ref[0] = fresh[:4].astype(jnp.bfloat16)
    fresh_ref[1] = fresh[4:].astype(jnp.bfloat16)
    fresh = fresh.astype(jnp.bfloat16)
    contract = (((1,), (1,)), ((), ()))
    score = lax.dot_general(
        heads_ref[...], fresh[:, :HD], contract, preferred_element_type=jnp.float32
    ) * (1.0 / math.sqrt(HD))
    score = jnp.where(mask_ref[...] == 0, score, jnp.float32(-1e30))
    old_peak = peak_ref[...]
    peak = jnp.maximum(old_peak, jnp.max(score, axis=1, keepdims=True))
    keep = jnp.exp(old_peak - peak)
    expo = jnp.exp(score - peak[:, :8])
    total = total_ref[...] * keep + jnp.sum(expo, axis=1, keepdims=True)
    mixed = jnp.dot(expo.astype(jnp.bfloat16), fresh[:, HD:], preferred_element_type=jnp.float32)
    mixed = (acc_ref[...] * keep + mixed) / total
    for j in range(GROUP):
        block = mixed[8 * j : 8 * j + 8]
        out_ref[0, :, HD * j : HD * (j + 1)] = block[:4].astype(jnp.bfloat16)
        out_ref[1, :, HD * j : HD * (j + 1)] = block[4:].astype(jnp.bfloat16)


def shape(sizes, dtype):
    return jax.ShapeDtypeStruct(sizes, dtype)


def local(
    master, moment_one, moment_two, gradient, hidden, queries, cache_keys, cache_values, lengths
):
    f32, bf16 = jnp.float32, jnp.bfloat16
    moved = lax.ppermute(hidden, LEARN + TP, HOPS)

    def adamw(master, moment_one, moment_two, gradient):
        grads = gradient.astype(f32)
        new_moment_one = beta_one * moment_one + (1.0 - beta_one) * grads
        new_moment_two = beta_two * moment_two + (1.0 - beta_two) * grads * grads
        update = new_moment_one / correct_one / (jnp.sqrt(new_moment_two / correct_two) + epsilon)
        new_master = master - learning_rate * (update + weight_decay * master)
        return new_master, new_moment_one, new_moment_two

    mask = pl.pallas_call(
        mask_kernel,
        out_shape=shape((64, 8), f32),
        out_specs=VMEM,
        compiler_params=PARAMS,
        cost_estimate=pl.CostEstimate(
            flops=4 * 64 * 4096 * 128, bytes_accessed=1 << 22, transcendentals=64 * 2048
        ),
        name="mask",
    )()
    state, mask = lax.optimization_barrier(((master, moment_one, moment_two, gradient), mask))
    weights = adamw(*state)[0].astype(bf16)
    weights = lax.all_gather(weights, REP, axis=0, tiled=True)
    moved, weights = lax.optimization_barrier((moved, weights))
    others = lax.ppermute(weights, "zlow", [(0, 1), (1, 0)])
    slots = pl.pallas_call(
        slots_kernel,
        out_shape=shape((8, 8, 1024), bf16),
        in_specs=[VMEM],
        out_specs=VMEM,
        compiler_params=PARAMS,
        name="slots",
    )(moved)
    tokens = lax.all_to_all(slots, TP, 0, 0, axis_index_groups=[BLOCKS])
    parts = pl.pallas_call(
        project_kernel,
        out_shape=shape((8, 8, 256), f32),
        in_specs=[VMEM] * 3,
        out_specs=VMEM,
        compiler_params=PARAMS,
        name="project",
    )(tokens, weights, others)
    parts, queries, *state = lax.optimization_barrier(
        (parts, queries, master, moment_one, moment_two, gradient)
    )
    new_master, new_moment_one, new_moment_two = adamw(*state)
    parts = lax.all_to_all(parts, "zpair", 0, 0, axis_index_groups=[PAIRS])
    cached = pl.pallas_call(
        cache_kernel,
        out_shape=[shape((64, HD), bf16)] + [shape((64, HD), f32)] * 3,
        in_specs=[SMEM] + [VMEM] * 3,
        out_specs=[VMEM] * 4,
        compiler_params=PARAMS,
        cost_estimate=pl.CostEstimate(
            flops=4 * 64 * 4096 * 128, bytes_accessed=1 << 22, transcendentals=64 * 2048
        ),
        name="cache",
    )(lengths, queries, cache_keys, cache_values)
    fresh_kv, attended = pl.pallas_call(
        finish_kernel,
        out_shape=[shape((2, 4, 256), bf16), shape((2, 4, 1024), bf16)],
        in_specs=[VMEM] * 6,
        out_specs=[VMEM] * 2,
        compiler_params=PARAMS,
        name="finish",
    )(parts, mask, *cached)
    return new_master, new_moment_one, new_moment_two, fresh_kv, attended


def solution(mesh):
    fine = Mesh(mesh.devices.reshape(SIZES), AXES)
    square = P(ROWS, TP)
    rows = P(ROWS, None, TP)
    return jax.shard_map(
        local,
        mesh=fine,
        in_specs=(square, square, square, square, rows, rows, rows, rows, P(ROWS)),
        out_specs=(square, square, square, rows, rows),
        check_vma=False,
    )
```
